32 devices in a mesh: groups: 2 (over y), adapter: 8 (over z, x), tensor: 2 (over core).
Axes of the slice: x: 2, y: 2, z: 4, core: 2. Of those that a mesh axis runs over, the one named last changes fastest.
Arguments:
- hidden_state_rows: bfloat16 [2048, 8192], P(('groups', 'adapter'), 'tensor'), parts along dimension 0, may hold values from -6 to 6
- value_weight: bfloat16 [8192, 512], P('tensor'), may hold values from -0.0625 to 0.0625
- adapter_down_weight: bfloat16 [16, 8192, 64], P(('groups', 'adapter'), 'tensor'), parts along dimension 0, may hold values from -0.0625 to 0.0625
- adapter_up_weight: bfloat16 [16, 64, 512], P(('groups', 'adapter'), None, 'tensor'), parts along dimension 0, may hold values from -0.75 to 0.75
- request_adapter_index: int32 [2048], P(('groups', 'adapter')), parts along dimension 0, may hold values from 0 to 7, as said below
Outputs:
- value_out: bfloat16 [2048, 512], P(('groups', 'adapter'), 'tensor'), parts along dimension 0
The draws below stay inside these ranges and needn't reach their ends.
There are 2 independent parts, one for each index of `groups`. The reference program is written for one: setup_inputs(seed, part) draws one part's arguments, and reference() takes and returns one part's arrays. A program takes and returns all parts, laid end to end along the dimension named above; an argument that names none is the same for every part. Nothing has to cross between parts.
Inputs may be any that keep to these rules, and one draw needn't show every extreme that they name: `request_adapter_index`: within the rows of one device (aligned blocks of 128 rows) no adapter is named more than 17 times; one adapter, the same for every device, is named exactly 17 times in every block.
All inputs are finite; a program needn't handle non-finite values.
Results may differ from the reference program's by a relative error of at most 0.001.
Values may be sent and summed in bfloat16 or wider, within the bound.
A program may use at most 64 MiB of HBM per device.

```python
import jax
import jax.numpy as jnp
from jax import lax

MODEL_WIDTH = 8192
VALUE_WIDTH = 512
ADAPTER_RANK = 64
R_DEV = 128
ROWS = 1024
ADAPTER_COUNT = 8
MOST = 17
N_ADAPTER = 8


def draw_request_adapter_index(key, part):
    key = jax.random.fold_in(key, 11)
    home_key, coin_key, offset_key, order_key = jax.random.split(key, 4)
    hot_home = jax.random.randint(home_key, (), 0, N_ADAPTER)
    coin_flags = jax.random.randint(coin_key, (N_ADAPTER,), 0, 2)
    offset_keys = jax.random.split(offset_key, N_ADAPTER)
    offset_table = jax.vmap(lambda sub_key: jax.random.permutation(sub_key, N_ADAPTER - 1))(offset_keys)
    order_keys = jax.random.split(order_key, N_ADAPTER)
    order_table = jax.vmap(lambda sub_key: jax.random.permutation(sub_key, R_DEV))(order_keys)
    positions = jnp.arange(R_DEV, dtype=jnp.int32)
    drawn_pick = jnp.maximum(positions - MOST, 0) % (N_ADAPTER - 1)
    coin_pick = jnp.where(positions < 2 * MOST, 0, 1 + jnp.maximum(positions - 2 * MOST, 0) % (N_ADAPTER - 2))
    selected_rows = jnp.where(coin_flags[:, None] == 1, coin_pick[None, :], drawn_pick[None, :])
    offsets = jnp.take_along_axis(offset_table, selected_rows, axis=1)
    home_ids = jnp.where(positions[None, :] < MOST, hot_home, (hot_home + 1 + offsets) % N_ADAPTER)
    shuffled = jnp.take_along_axis(home_ids, order_table, axis=1)
    return shuffled.reshape(-1).astype(jnp.int32)


def steps_of(own_key, shape, pieces, low, largest):
    level = 1.0
    for position, parts in pieces:
        steps = jax.random.uniform(jax.random.fold_in(jax.random.fold_in(own_key, 6), position), (parts,), jnp.float32, low / len(pieces), largest / len(pieces))
        level = level * jnp.repeat(jnp.exp(steps), shape[position] // parts).reshape((-1,) + (1,) * (len(shape) - 1 - position))
    return level


def scatter_about(key, extent, width, limit, pieces=(), kind=jnp.bfloat16):
    values = jax.random.normal(key, extent, jnp.float32) * width
    if len(pieces) > 0:
        values = steps_of(key, extent, pieces, -0.22, 0.18) * values
    return jnp.clip(values, min=-limit, max=limit).astype(kind)


def setup_inputs(seed: int = 0, part: int = 0) -> dict:
    seeds = jax.random.split(jax.random.key(seed), 6)
    part_splits = jax.random.split(jax.random.fold_in(seeds[5], part), 6)
    hidden_state_rows = scatter_about(part_splits[0], (ROWS, MODEL_WIDTH), 1.0, 6.0, ((0, 8), (1, 2)))
    value_weight = scatter_about(seeds[1], (MODEL_WIDTH, VALUE_WIDTH), MODEL_WIDTH ** -0.5, 0.0625, ((0, 2),))
    adapter_down_weight = scatter_about(part_splits[2], (ADAPTER_COUNT, MODEL_WIDTH, ADAPTER_RANK), MODEL_WIDTH ** -0.5, 0.0625, ((0, 8), (1, 2)))
    adapter_up_weight = scatter_about(part_splits[3], (ADAPTER_COUNT, ADAPTER_RANK, VALUE_WIDTH), ADAPTER_RANK ** -0.5, 0.75, ((0, 8), (2, 2)))
    request_adapter_index = draw_request_adapter_index(jax.random.fold_in(jax.random.fold_in(seeds[5], part), 71), part)
    return dict(hidden_state_rows=hidden_state_rows, value_weight=value_weight, adapter_down_weight=adapter_down_weight, adapter_up_weight=adapter_up_weight, request_adapter_index=request_adapter_index)


highest_precision = lax.Precision.HIGHEST


def reference(hidden_state_rows, value_weight, adapter_down_weight, adapter_up_weight, request_adapter_index):
    base_terms = jnp.dot(hidden_state_rows, value_weight, preferred_element_type=jnp.float32)
    capacity = N_ADAPTER * MOST

    def one_adapter(delta_rows, adapter_slot):
        matches = request_adapter_index == adapter_slot
        chosen = jnp.nonzero(matches, size=capacity, fill_value=0)[0].astype(jnp.int32)
        counted = jnp.sum(matches.astype(jnp.int32))
        valid = jnp.arange(capacity, dtype=jnp.int32) < counted
        selected_rows = jnp.take(hidden_state_rows, chosen, axis=0)
        reduced_rows = jnp.dot(selected_rows, adapter_down_weight[adapter_slot], preferred_element_type=jnp.float32)
        widened_rows = jnp.dot(reduced_rows, adapter_up_weight[adapter_slot].astype(jnp.float32), precision=highest_precision, preferred_element_type=jnp.float32)
        widened_rows = jnp.where(valid[:, None], widened_rows, jnp.zeros_like(widened_rows))
        return delta_rows.at[chosen].add(widened_rows), counted

    start_rows = jnp.zeros((ROWS, VALUE_WIDTH), jnp.float32)
    delta_rows, unused = lax.scan(one_adapter, start_rows, jnp.arange(ADAPTER_COUNT, dtype=jnp.int32))
    return (base_terms + delta_rows).astype(jnp.bfloat16)
```

```python
import functools

import jax
import jax.numpy as jnp
from jax import lax
from jax.experimental import pallas as pl
from jax.experimental.pallas import tpu as pltpu
from jax.sharding import PartitionSpec as P

highest_precision = lax.Precision.HIGHEST
BLOCK = 16
f32 = jnp.float32
bf16 = jnp.bfloat16


def dot(a, b):
    return jnp.dot(a, b, preferred_element_type=f32)


def three_parts(x):
    high = x.astype(bf16)
    rest = x - high.astype(f32)
    middle = rest.astype(bf16)
    low = (rest - middle.astype(f32)).astype(bf16)
    return high, middle, low


def adapter_kernel(
    n, groups, index_ref, hidden_hbm, value_hbm, down_hbm, up_hbm, out_ref,
    hidden, value, down, up, rows_out, rows_in, spill_out, spill_in,
    part_out, part_in, delta_out, delta_in, spill_delta_out, spill_delta_in,
    base_own, base_out, base_in,
    load_sem, rows_sem, spill_sem, part_sem, delta_sem, spill_delta_sem, base_sem,
):
    me = lax.axis_index("adapter")
    core = lax.axis_index("tensor")
    rows, depth = hidden.shape
    width = value.shape[1]
    half = width // 2
    rank = up.shape[0]
    chunks = depth // 128

    loads = [
        pltpu.make_async_copy(src, dst, load_sem.at[i])
        for i, (src, dst) in enumerate(
            ((hidden_hbm, hidden), (down_hbm, down), (up_hbm, up), (value_hbm, value))
        )
    ]
    for load in loads:
        load.start()

    barrier = pltpu.get_barrier_semaphore()
    for k in range(1, n):
        pl.semaphore_signal(barrier, inc=1, device_id={"adapter": me ^ k})
    pl.semaphore_signal(barrier, inc=1, device_id={"tensor": 1 - core})

    def push(src, dst, sems, k, target):
        copy = pltpu.make_async_remote_copy(
            src_ref=src, dst_ref=dst, send_sem=sems.at[0, k], recv_sem=sems.at[1, k],
            device_id=target,
        )
        copy.start()
        return copy

    block_of = index_ref[...] ^ me
    member = (lax.broadcasted_iota(jnp.int32, (n, rows), 0) == block_of).astype(f32)
    earlier = (
        lax.broadcasted_iota(jnp.int32, (rows, rows), 0)
        < lax.broadcasted_iota(jnp.int32, (rows, rows), 1)
    ).astype(bf16)
    place = jnp.sum(member * dot(member.astype(bf16), earlier), axis=0, keepdims=True)
    place = place.astype(jnp.int32)
    main_slot = jnp.where(place < BLOCK, block_of * BLOCK + place, -1)
    spill_block = jnp.where(place == BLOCK, block_of, -1)
    main_pick = lax.broadcasted_iota(jnp.int32, (n * BLOCK, rows), 0) == main_slot
    spill_pick = lax.broadcasted_iota(jnp.int32, (n, rows), 0) == spill_block
    pick = jnp.concatenate([main_pick.astype(f32), spill_pick.astype(f32)], axis=0).astype(bf16)
    eighth = lax.broadcasted_iota(jnp.int32, (n * 8, rows), 0)
    back = jnp.concatenate(
        [
            main_pick.astype(f32),
            (eighth == spill_block * 8).astype(f32),
            (eighth == spill_block * 8 + 1).astype(f32),
        ],
        axis=0,
    )
    back = jnp.transpose(back).astype(bf16)
    turn_row = lax.broadcasted_iota(jnp.int32, (n * chunks, n * chunks), 0)
    turn_column = lax.broadcasted_iota(jnp.int32, (n * chunks, n * chunks), 1)

    loads[0].wait()
    picked = dot(pick, hidden[...])
    rows_out[...] = picked[: n * BLOCK].astype(bf16).reshape(n, BLOCK, depth)
    turn = (turn_row % chunks * n + turn_row // chunks == turn_column).astype(bf16)
    spilled = jnp.concatenate(
        [picked[n * BLOCK :, c * 128 : (c + 1) * 128] for c in range(chunks)], axis=0
    ).astype(bf16)
    spill_out[...] = dot(turn, spilled).astype(bf16).reshape(n, chunks, 128)

    pl.semaphore_wait(barrier, n)
    spill_copies = {}
    row_copies = {}
    for k in range(1, n):
        spill_copies[k] = push(
            spill_out.at[k], spill_in.at[k], spill_sem, k, {"adapter": me ^ k}
        )
    for k in [k for group in groups for k in group if k > 0]:
        row_copies[k] = push(rows_out.at[k], rows_in.at[k], rows_sem, k, {"adapter": me ^ k})

    loads[3].wait()
    base = dot(hidden[...], value[...])
    first, second = base[:, :half], base[:, half:]
    base_own[...] = jnp.where(core == 0, first, second)
    base_out[...] = jnp.where(core == 0, second, first)
    base_copy = push(base_out, base_in, base_sem, 0, {"tensor": 1 - core})

    loads[1].wait()
    loads[2].wait()
    rows_in[0] = rows_out[0]
    spill_in[0] = spill_out[0]

    def shrink_part(block):
        part = dot(block, down[...])
        return jnp.concatenate([part, jnp.zeros((part.shape[0], 128 - rank), f32)], axis=1)

    def widen(reduced):
        count = reduced.shape[0]
        stacked = jnp.concatenate([x.astype(f32) for x in three_parts(reduced)], axis=0)
        wide = dot(stacked.astype(bf16), up[...])
        return wide[:count] + wide[count : 2 * count] + wide[2 * count :]

    part_copies = []
    delta_copies = []
    spill_delta_copies = []

    def exchange(start, count, slot):
        region = pl.ds(start, count)
        copy = push(part_out.at[region], part_in.at[region], part_sem, slot, {"tensor": 1 - core})
        part_copies.append(copy)
        copy.wait_recv()
        return (part_out[region] + part_in[region])[:, :rank]

    for g, group in enumerate(groups):
        for k in group:
            if k > 0:
                row_copies[k].wait_recv()
        begin, count = group[0] * BLOCK, len(group) * BLOCK
        block = rows_in[group[0] : group[0] + len(group)].reshape(count, depth)
        part_out[pl.ds(begin, count)] = shrink_part(block)
        deltas = widen(exchange(begin, count, g)).reshape(len(group), BLOCK, half)
        for i, k in enumerate(group):
            if k == 0:
                delta_in[0] = deltas[i]
            else:
                delta_out[k] = deltas[i]
                delta_copies.append(
                    push(delta_out.at[k], delta_in.at[k], delta_sem, k, {"adapter": me ^ k})
                )
        if g == 0:
            for k in range(1, n):
                spill_copies[k].wait_recv()
            turn_back = (turn_row % n * chunks + turn_row // n == turn_column).astype(bf16)
            turned = dot(turn_back, spill_in[...].reshape(n * chunks, 128))
            spilled = jnp.concatenate(
                [turned[c * n : (c + 1) * n] for c in range(chunks)], axis=1
            ).astype(bf16)
            part_out[pl.ds(n * BLOCK, n)] = shrink_part(spilled)
            wide = widen(exchange(n * BLOCK, n, len(groups)))
            spill_delta_out[...] = jnp.zeros_like(spill_delta_out)
            for k in range(n):
                spill_delta_out[k, 0:1, :] = wide[k : k + 1, :128]
                spill_delta_out[k, 1:2, :] = wide[k : k + 1, 128:]
            spill_delta_in[0] = spill_delta_out[0]
            for k in range(1, n):
                spill_delta_copies.append(
                    push(
                        spill_delta_out.at[k], spill_delta_in.at[k], spill_delta_sem, k,
                        {"adapter": me ^ k},
                    )
                )

    base_copy.wait_recv()
    total = base_own[...] + base_in[...]
    for copy in spill_delta_copies:
        copy.wait_recv()
    spill_deltas = spill_delta_in[...].reshape(n * 8, 128)
    low = sum(dot(back[:, n * BLOCK : n * BLOCK + n * 8], x) for x in three_parts(spill_deltas))
    high = sum(dot(back[:, n * BLOCK + n * 8 :], x) for x in three_parts(spill_deltas))
    total = total + jnp.concatenate([low, high], axis=1)
    for copy in delta_copies:
        copy.wait_recv()
    deltas = delta_in[...].reshape(n * BLOCK, half)
    total = total + sum(dot(back[:, : n * BLOCK], x) for x in three_parts(deltas))
    out_ref[...] = total.astype(out_ref.dtype)

    for copy in [*spill_copies.values(), *row_copies.values(), *part_copies, *delta_copies,
                 *spill_delta_copies, base_copy]:
        copy.wait_send()


def fused_body(
    hidden_state_rows, value_weight, adapter_down_weight, adapter_up_weight, request_adapter_index
):
    n = lax.axis_size("adapter")
    rows, depth = hidden_state_rows.shape
    width = value_weight.shape[1]
    half = width // 2
    rank = adapter_down_weight.shape[2]
    chunks = depth // 128
    groups = GROUPS
    dma = pltpu.SemaphoreType.DMA
    return pl.pallas_call(
        functools.partial(adapter_kernel, n, groups),
        out_shape=jax.ShapeDtypeStruct((rows, half), bf16),
        in_specs=[pl.BlockSpec(memory_space=pltpu.VMEM)]
        + [pl.BlockSpec(memory_space=pl.ANY)] * 4,
        out_specs=pl.BlockSpec(memory_space=pltpu.VMEM),
        scratch_shapes=[
            pltpu.VMEM((rows, depth), bf16),
            pltpu.VMEM((depth, width), bf16),
            pltpu.VMEM((depth, rank), bf16),
            pltpu.VMEM((rank, half), bf16),
            pltpu.VMEM((n, BLOCK, depth), bf16),
            pltpu.VMEM((n, BLOCK, depth), bf16),
            pltpu.VMEM((n, chunks, 128), bf16),
            pltpu.VMEM((n, chunks, 128), bf16),
            pltpu.VMEM((n * BLOCK + n, 128), f32),
            pltpu.VMEM((n * BLOCK + n, 128), f32),
            pltpu.VMEM((n, BLOCK, half), f32),
            pltpu.VMEM((n, BLOCK, half), f32),
            pltpu.VMEM((n, 8, 128), f32),
            pltpu.VMEM((n, 8, 128), f32),
            pltpu.VMEM((rows, half), f32),
            pltpu.VMEM((rows, half), f32),
            pltpu.VMEM((rows, half), f32),
            dma((4,)),
            dma((2, n)),
            dma((2, n)),
            dma((2, n + 1)),
            dma((2, n)),
            dma((2, n)),
            dma((2, 1)),
        ],
        compiler_params=pltpu.CompilerParams(
            collective_id=0, has_side_effects=True, vmem_limit_bytes=40 * 1024 * 1024
        ),
    )(
        request_adapter_index.reshape(1, rows),
        hidden_state_rows,
        value_weight,
        adapter_down_weight.reshape(depth, rank),
        adapter_up_weight.reshape(rank, half),
    )


GROUPS = ((0, 1), (2, 3), (4, 5), (6, 7))


def adapter_delta_rows(incoming_rows, down_matrix, up_matrix):
    flat_rows = incoming_rows.reshape(-1, incoming_rows.shape[-1])
    reduced_rows = jnp.dot(flat_rows, down_matrix, preferred_element_type=jnp.float32)
    reduced_rows = lax.psum(reduced_rows, "tensor")
    widened_rows = jnp.dot(
        reduced_rows, up_matrix, precision=highest_precision, preferred_element_type=jnp.float32
    )
    widened_rows = widened_rows.reshape(
        incoming_rows.shape[0], incoming_rows.shape[1], up_matrix.shape[1]
    )
    return lax.all_to_all(widened_rows, "adapter", split_axis=0, concat_axis=0, tiled=True)


def general_body(
    hidden_state_rows, value_weight, adapter_down_weight, adapter_up_weight, request_adapter_index
):
    holders = lax.axis_size("adapter")
    rows_here = hidden_state_rows.shape[0]
    slots_per_pair = 2 + (rows_here - 1) // holders
    holder_ids = lax.broadcasted_iota(jnp.int32, (rows_here, holders), 1)
    onehot = (request_adapter_index[:, None] == holder_ids).astype(jnp.int32)
    pair_ranks = jnp.sum(onehot * (jnp.cumsum(onehot, axis=0) - 1), axis=1)
    slot_index = request_adapter_index * slots_per_pair + pair_ranks
    down_matrix = adapter_down_weight[0]
    up_matrix = adapter_up_weight[0].astype(jnp.float32)
    slot_ids = lax.broadcasted_iota(jnp.int32, (holders * slots_per_pair, rows_here), 0)
    placing = (slot_ids == slot_index[None, :]).astype(hidden_state_rows.dtype)
    send_rows = jnp.dot(placing, hidden_state_rows, preferred_element_type=jnp.float32).astype(
        hidden_state_rows.dtype
    )
    send_rows = send_rows.reshape(holders, slots_per_pair, hidden_state_rows.shape[1])
    value_result = adapter_delta_rows(
        lax.all_to_all(send_rows, "adapter", split_axis=0, concat_axis=0, tiled=True),
        down_matrix,
        up_matrix,
    )
    delta_rows = jnp.take(value_result.reshape(holders * slots_per_pair, -1), slot_index, axis=0)
    base_terms = jnp.dot(hidden_state_rows, value_weight, preferred_element_type=jnp.float32)
    own_columns = lax.psum_scatter(base_terms, "tensor", scatter_dimension=1, tiled=True)
    summed = own_columns + delta_rows
    return summed.astype(jnp.bfloat16)


def body(*arrays):
    n = lax.axis_size("adapter")
    if n == 8 and arrays[0].shape[0] == n * BLOCK:
        return fused_body(*arrays)
    return general_body(*arrays)


def solution(mesh):
    return jax.shard_map(
        body,
        mesh=mesh,
        in_specs=(
            P(("groups", "adapter"), "tensor"),
            P("tensor", None),
            P(("groups", "adapter"), "tensor", None),
            P(("groups", "adapter"), None, "tensor"),
            P(("groups", "adapter")),
        ),
        out_specs=P(("groups", "adapter"), "tensor"),
        check_vma=False,
    )
```

```python
import functools

import jax
import jax.numpy as jnp
from jax import lax
from jax.experimental import pallas as pl
from jax.experimental.pallas import tpu as pltpu
from jax.sharding import PartitionSpec as P

highest_precision = lax.Precision.HIGHEST
BLOCK = 16
f32 = jnp.float32
bf16 = jnp.bfloat16


def dot(a, b):
    return jnp.dot(a, b, preferred_element_type=f32)


def three_parts(x):
    high = x.astype(bf16)
    rest = x - high.astype(f32)
    middle = rest.astype(bf16)
    low = (rest - middle.astype(f32)).astype(bf16)
    return high, middle, low


def adapter_kernel(
    n, groups, index_hbm, hidden_hbm, value_hbm, down_hbm, up_hbm, out_ref,
    index, hidden, value, down, up, rows_out, rows_in, spill_out, spill_in,
    part_out, part_in, delta_out, delta_in, spill_delta_out, spill_delta_in,
    base_own, base_out, base_in,
    load_sem, rows_sem, spill_sem, part_sem, delta_sem, spill_delta_sem, base_sem,
):
    me = lax.axis_index("adapter")
    core = lax.axis_index("tensor")
    rows, depth = hidden.shape
    width = value.shape[1]
    half = width // 2
    rank = up.shape[0]
    chunks = depth // 128

    loads = [
        pltpu.make_async_copy(src, dst, load_sem.at[i])
        for i, (src, dst) in enumerate(
            (
                (index_hbm, index), (hidden_hbm, hidden), (down_hbm, down), (up_hbm, up),
                (value_hbm, value),
            )
        )
    ]
    for load in loads:
        load.start()

    barrier = pltpu.get_barrier_semaphore()
    for k in range(1, n):
        pl.semaphore_signal(barrier, inc=1, device_id={"adapter": me ^ k})
    pl.semaphore_signal(barrier, inc=1, device_id={"tensor": 1 - core})

    def push(src, dst, sems, k, target):
        copy = pltpu.make_async_remote_copy(
            src_ref=src, dst_ref=dst, send_sem=sems.at[0, k], recv_sem=sems.at[1, k],
            device_id=target,
        )
        copy.start()
        return copy

    loads[0].wait()
    block_of = index[...] ^ me
    member = (lax.broadcasted_iota(jnp.int32, (n, rows), 0) == block_of).astype(f32)
    earlier = (
        lax.broadcasted_iota(jnp.int32, (rows, rows), 0)
        < lax.broadcasted_iota(jnp.int32, (rows, rows), 1)
    ).astype(bf16)
    place = jnp.sum(member * dot(member.astype(bf16), earlier), axis=0, keepdims=True)
    place = place.astype(jnp.int32)
    main_slot = jnp.where(place < BLOCK, block_of * BLOCK + place, -1)
    spill_block = jnp.where(place == BLOCK, block_of, -1)
    main_pick = lax.broadcasted_iota(jnp.int32, (n * BLOCK, rows), 0) == main_slot
    spill_pick = lax.broadcasted_iota(jnp.int32, (n, rows), 0) == spill_block
    pick = jnp.concatenate([main_pick.astype(f32), spill_pick.astype(f32)], axis=0).astype(bf16)
    eighth = lax.broadcasted_iota(jnp.int32, (n * 8, rows), 0)
    back = jnp.concatenate(
        [
            main_pick.astype(f32),
            (eighth == spill_block * 8).astype(f32),
            (eighth == spill_block * 8 + 1).astype(f32),
        ],
        axis=0,
    )
    back = jnp.transpose(back).astype(bf16)
    turn_row = lax.broadcasted_iota(jnp.int32, (n * chunks, n * chunks), 0)
    turn_column = lax.broadcasted_iota(jnp.int32, (n * chunks, n * chunks), 1)

    loads[1].wait()
    picked = dot(pick, hidden[...])
    rows_out[...] = picked[: n * BLOCK].astype(bf16).reshape(n, BLOCK, depth)
    turn = (turn_row % chunks * n + turn_row // chunks == turn_column).astype(bf16)
    spilled = jnp.concatenate(
        [picked[n * BLOCK :, c * 128 : (c + 1) * 128] for c in range(chunks)], axis=0
    ).astype(bf16)
    spill_out[...] = dot(turn, spilled).astype(bf16).reshape(n, chunks, 128)

    pl.semaphore_wait(barrier, n)
    spill_copies = {}
    row_copies = {}
    for k in range(1, n):
        spill_copies[k] = push(
            spill_out.at[k], spill_in.at[k], spill_sem, k, {"adapter": me ^ k}
        )
    for k in [k for group in groups for k in group if k > 0]:
        row_copies[k] = push(rows_out.at[k], rows_in.at[k], rows_sem, k, {"adapter": me ^ k})

    loads[4].wait()
    base = dot(hidden[...], value[...])
    first, second = base[:, :half], base[:, half:]
    base_own[...] = jnp.where(core == 0, first, second)
    base_out[...] = jnp.where(core == 0, second, first)
    base_copy = push(base_out, base_in, base_sem, 0, {"tensor": 1 - core})

    loads[2].wait()
    loads[3].wait()
    rows_in[0] = rows_out[0]
    spill_in[0] = spill_out[0]

    def shrink_part(block):
        part = lax.dot_general(
            block, down[...], (((1,), (1,)), ((), ())), preferred_element_type=f32
        )
        return jnp.concatenate([part, jnp.zeros((part.shape[0], 128 - rank), f32)], axis=1)

    def widen(reduced):
        count = reduced.shape[0]
        stacked = jnp.concatenate([x.astype(f32) for x in three_parts(reduced)], axis=0)
        wide = dot(stacked.astype(bf16), up[...])
        return wide[:count] + wide[count : 2 * count] + wide[2 * count :]

    part_copies = []
    delta_copies = []
    spill_delta_copies = []

    def exchange(start, count, slot):
        region = pl.ds(start, count)
        copy = push(part_out.at[region], part_in.at[region], part_sem, slot, {"tensor": 1 - core})
        part_copies.append(copy)
        copy.wait_recv()
        return (part_out[region] + part_in[region])[:, :rank]

    for g, group in enumerate(groups):
        for k in group:
            if k > 0:
                row_copies[k].wait_recv()
        begin, count = group[0] * BLOCK, len(group) * BLOCK
        block = rows_in[group[0] : group[0] + len(group)].reshape(count, depth)
        part_out[pl.ds(begin, count)] = shrink_part(block)
        deltas = widen(exchange(begin, count, g)).reshape(len(group), BLOCK, half)
        for i, k in enumerate(group):
            if k == 0:
                delta_in[0] = deltas[i]
            else:
                delta_out[k] = deltas[i]
                delta_copies.append(
                    push(delta_out.at[k], delta_in.at[k], delta_sem, k, {"adapter": me ^ k})
                )
        if g == 0:
            for k in range(1, n):
                spill_copies[k].wait_recv()
            turn_back = (turn_row % n * chunks + turn_row // n == turn_column).astype(bf16)
            turned = dot(turn_back, spill_in[...].reshape(n * chunks, 128))
            spilled = jnp.concatenate(
                [turned[c * n : (c + 1) * n] for c in range(chunks)], axis=1
            ).astype(bf16)
            part_out[pl.ds(n * BLOCK, n)] = shrink_part(spilled)
            wide = widen(exchange(n * BLOCK, n, len(groups)))
            spill_delta_out[...] = jnp.zeros_like(spill_delta_out)
            for k in range(n):
                spill_delta_out[k, 0:1, :] = wide[k : k + 1, :128]
                spill_delta_out[k, 1:2, :] = wide[k : k + 1, 128:]
            spill_delta_in[0] = spill_delta_out[0]
            for k in range(1, n):
                spill_delta_copies.append(
                    push(
                        spill_delta_out.at[k], spill_delta_in.at[k], spill_delta_sem, k,
                        {"adapter": me ^ k},
                    )
                )

    base_copy.wait_recv()
    total = base_own[...] + base_in[...]
    for copy in spill_delta_copies:
        copy.wait_recv()
    spill_deltas = spill_delta_in[...].reshape(n * 8, 128)
    low = sum(dot(back[:, n * BLOCK : n * BLOCK + n * 8], x) for x in three_parts(spill_deltas))
    high = sum(dot(back[:, n * BLOCK + n * 8 :], x) for x in three_parts(spill_deltas))
    total = total + jnp.concatenate([low, high], axis=1)
    for copy in delta_copies:
        copy.wait_recv()
    deltas = delta_in[...].reshape(n * BLOCK, half)
    total = total + sum(dot(back[:, : n * BLOCK], x) for x in three_parts(deltas))
    out_ref[...] = total.astype(out_ref.dtype)

    for copy in [*spill_copies.values(), *row_copies.values(), *part_copies, *delta_copies,
                 *spill_delta_copies, base_copy]:
        copy.wait_send()


def fused_body(
    hidden_state_rows, value_weight, adapter_down_weight, adapter_up_weight, request_adapter_index
):
    n = lax.axis_size("adapter")
    rows, depth = hidden_state_rows.shape
    width = value_weight.shape[1]
    half = width // 2
    rank = adapter_down_weight.shape[2]
    chunks = depth // 128
    groups = GROUPS
    dma = pltpu.SemaphoreType.DMA
    return pl.pallas_call(
        functools.partial(adapter_kernel, n, groups),
        out_shape=jax.ShapeDtypeStruct((rows, half), bf16),
        in_specs=[pl.BlockSpec(memory_space=pl.ANY)] * 5,
        out_specs=pl.BlockSpec(memory_space=pltpu.VMEM),
        scratch_shapes=[
            pltpu.VMEM((1, rows), jnp.int32),
            pltpu.VMEM((rows, depth), bf16),
            pltpu.VMEM((depth, width), bf16),
            pltpu.VMEM((rank, depth), bf16),
            pltpu.VMEM((rank, half), bf16),
            pltpu.VMEM((n, BLOCK, depth), bf16),
            pltpu.VMEM((n, BLOCK, depth), bf16),
            pltpu.VMEM((n, chunks, 128), bf16),
            pltpu.VMEM((n, chunks, 128), bf16),
            pltpu.VMEM((n * BLOCK + n, 128), f32),
            pltpu.VMEM((n * BLOCK + n, 128), f32),
            pltpu.VMEM((n, BLOCK, half), f32),
            pltpu.VMEM((n, BLOCK, half), f32),
            pltpu.VMEM((n, 8, 128), f32),
            pltpu.VMEM((n, 8, 128), f32),
            pltpu.VMEM((rows, half), f32),
            pltpu.VMEM((rows, half), f32),
            pltpu.VMEM((rows, half), f32),
            dma((5,)),
            dma((2, n)),
            dma((2, n)),
            dma((2, n + 1)),
            dma((2, n)),
            dma((2, n)),
            dma((2, 1)),
        ],
        compiler_params=pltpu.CompilerParams(
            collective_id=0, has_side_effects=True, vmem_limit_bytes=60 * 1024 * 1024
        ),
    )(
        request_adapter_index.reshape(1, rows),
        hidden_state_rows,
        value_weight,
        jnp.swapaxes(adapter_down_weight.reshape(depth, rank), 0, 1),
        adapter_up_weight.reshape(rank, half),
    )


GROUPS = ((0, 1), (2, 3), (4, 5), (6, 7))


def adapter_delta_rows(incoming_rows, down_matrix, up_matrix):
    flat_rows = incoming_rows.reshape(-1, incoming_rows.shape[-1])
    reduced_rows = jnp.dot(flat_rows, down_matrix, preferred_element_type=jnp.float32)
    reduced_rows = lax.psum(reduced_rows, "tensor")
    widened_rows = jnp.dot(
        reduced_rows, up_matrix, precision=highest_precision, preferred_element_type=jnp.float32
    )
    widened_rows = widened_rows.reshape(
        incoming_rows.shape[0], incoming_rows.shape[1], up_matrix.shape[1]
    )
    return lax.all_to_all(widened_rows, "adapter", split_axis=0, concat_axis=0, tiled=True)


def general_body(
    hidden_state_rows, value_weight, adapter_down_weight, adapter_up_weight, request_adapter_index
):
    holders = lax.axis_size("adapter")
    rows_here = hidden_state_rows.shape[0]
    slots_per_pair = 2 + (rows_here - 1) // holders
    holder_ids = lax.broadcasted_iota(jnp.int32, (rows_here, holders), 1)
    onehot = (request_adapter_index[:, None] == holder_ids).astype(jnp.int32)
    pair_ranks = jnp.sum(onehot * (jnp.cumsum(onehot, axis=0) - 1), axis=1)
    slot_index = request_adapter_index * slots_per_pair + pair_ranks
    down_matrix = adapter_down_weight[0]
    up_matrix = adapter_up_weight[0].astype(jnp.float32)
    slot_ids = lax.broadcasted_iota(jnp.int32, (holders * slots_per_pair, rows_here), 0)
    placing = (slot_ids == slot_index[None, :]).astype(hidden_state_rows.dtype)
    send_rows = jnp.dot(placing, hidden_state_rows, preferred_element_type=jnp.float32).astype(
        hidden_state_rows.dtype
    )
    send_rows = send_rows.reshape(holders, slots_per_pair, hidden_state_rows.shape[1])
    value_result = adapter_delta_rows(
        lax.all_to_all(send_rows, "adapter", split_axis=0, concat_axis=0, tiled=True),
        down_matrix,
        up_matrix,
    )
    delta_rows = jnp.take(value_result.reshape(holders * slots_per_pair, -1), slot_index, axis=0)
    base_terms = jnp.dot(hidden_state_rows, value_weight, preferred_element_type=jnp.float32)
    own_columns = lax.psum_scatter(base_terms, "tensor", scatter_dimension=1, tiled=True)
    summed = own_columns + delta_rows
    return summed.astype(jnp.bfloat16)


def body(*arrays):
    n = lax.axis_size("adapter")
    if n == 8 and arrays[0].shape[0] == n * BLOCK:
        return fused_body(*arrays)
    return general_body(*arrays)


def solution(mesh):
    return jax.shard_map(
        body,
        mesh=mesh,
        in_specs=(
            P(("groups", "adapter"), "tensor"),
            P("tensor", None),
            P(("groups", "adapter"), "tensor", None),
            P(("groups", "adapter"), None, "tensor"),
            P(("groups", "adapter")),
        ),
        out_specs=P(("groups", "adapter"), "tensor"),
        check_vma=False,
    )
```

```python
import functools

import jax
import jax.numpy as jnp
from jax import lax
from jax.experimental import pallas as pl
from jax.experimental.pallas import tpu as pltpu
from jax.sharding import PartitionSpec as P

highest_precision = lax.Precision.HIGHEST
BLOCK = 16
f32 = jnp.float32
bf16 = jnp.bfloat16


def dot(a, b):
    return jnp.dot(a, b, preferred_element_type=f32)


def three_parts(x):
    high = x.astype(bf16)
    rest = x - high.astype(f32)
    middle = rest.astype(bf16)
    low = (rest - middle.astype(f32)).astype(bf16)
    return high, middle, low


def adapter_kernel(
    n, groups, index_hbm, hidden_hbm, value_hbm, down_hbm, up_hbm, out_ref,
    index, hidden, value, down, up, rows_out, rows_in, part_out, part_in, delta_out, delta_in,
    base_own, base_out, base_in,
    load_sem, rows_sem, part_sem, delta_sem, base_sem,
):
    me = lax.axis_index("adapter")
    core = lax.axis_index("tensor")
    rows, depth = hidden.shape
    width = value.shape[1]
    half = width // 2
    rank = up.shape[0]
    chunks = depth // 128
    main = chunks * BLOCK
    each = len(groups[0])
    count = each * BLOCK

    loads = [
        pltpu.make_async_copy(src, dst, load_sem.at[i])
        for i, (src, dst) in enumerate(
            (
                (index_hbm, index), (hidden_hbm, hidden), (down_hbm, down), (up_hbm, up),
                (value_hbm, value),
            )
        )
    ]
    loads[0].start()
    loads[1].start()

    barrier = pltpu.get_barrier_semaphore()
    for k in range(1, n):
        pl.semaphore_signal(barrier, inc=1, device_id={"adapter": me ^ k})
    pl.semaphore_signal(barrier, inc=1, device_id={"tensor": 1 - core})

    sent = []

    def push(src, dst, sems, k, target):
        copy = pltpu.make_async_remote_copy(
            src_ref=src, dst_ref=dst, send_sem=sems.at[0, k], recv_sem=sems.at[1, k],
            device_id=target,
        )
        copy.start()
        sent.append(copy)
        return copy

    loads[0].wait()
    block_of = index[...] ^ me
    member = (lax.broadcasted_iota(jnp.int32, (n, rows), 0) == block_of).astype(f32)
    earlier = (
        lax.broadcasted_iota(jnp.int32, (rows, rows), 0)
        < lax.broadcasted_iota(jnp.int32, (rows, rows), 1)
    ).astype(bf16)
    place = jnp.sum(member * dot(member.astype(bf16), earlier), axis=0, keepdims=True)
    place = place.astype(jnp.int32)
    main_slot = jnp.where(place < BLOCK, block_of * BLOCK + place, -1)
    spill_block = jnp.where(place == BLOCK, block_of, -1)
    main_pick = lax.broadcasted_iota(jnp.int32, (n * BLOCK, rows), 0) == main_slot
    spill_pick = lax.broadcasted_iota(jnp.int32, (n, rows), 0) == spill_block
    pick = jnp.concatenate([main_pick.astype(f32), spill_pick.astype(f32)], axis=0).astype(bf16)
    turn_row = lax.broadcasted_iota(jnp.int32, (n * chunks, n * chunks), 0)
    turn_column = lax.broadcasted_iota(jnp.int32, (n * chunks, n * chunks), 1)
    turn = (turn_row % chunks * n + turn_row // chunks == turn_column).astype(bf16)

    loads[1].wait()
    for load in loads[2:]:
        load.start()
    picked = dot(pick, hidden[...])
    for c in range(chunks):
        rows_out[:, c * BLOCK : (c + 1) * BLOCK, :] = (
            picked[: n * BLOCK, c * 128 : (c + 1) * 128].astype(bf16).reshape(n, BLOCK, 128)
        )
    spilled = jnp.concatenate(
        [picked[n * BLOCK :, c * 128 : (c + 1) * 128] for c in range(chunks)], axis=0
    ).astype(bf16)
    rows_out[:, main:, :] = dot(turn, spilled).astype(bf16).reshape(n, chunks, 128)

    pl.semaphore_wait(barrier, n)
    row_copies = {}
    for k in range(1, n):
        row_copies[k] = push(rows_out.at[k], rows_in.at[k], rows_sem, k, {"adapter": me ^ k})

    loads[4].wait()
    base = dot(hidden[...], value[...])
    first, second = base[:, :half], base[:, half:]
    base_own[...] = jnp.where(core == 0, first, second)
    base_out[...] = jnp.where(core == 0, second, first)
    base_copy = push(base_out, base_in, base_sem, 0, {"tensor": 1 - core})

    rows_in[0] = rows_out[0]
    delta_out[...] = jnp.zeros_like(delta_out)
    low_slot = jnp.where(place < BLOCK, place, 2 * BLOCK) + block_of * SLOTS
    high_slot = jnp.where(place < BLOCK, BLOCK + place, 2 * BLOCK + 1) + block_of * SLOTS
    slot_ids = lax.broadcasted_iota(jnp.int32, (128, rows), 0)
    backs = []
    for group in groups:
        slots = jnp.where(slot_ids < each * SLOTS, slot_ids + group[0] * SLOTS, -1)
        backs.append(
            [
                jnp.transpose((slots == slot).astype(f32))[:, : each * SLOTS].astype(bf16)
                for slot in (low_slot, high_slot)
            ]
        )
    gather_row = lax.broadcasted_iota(jnp.int32, (8 * chunks, each * chunks), 0)
    gather_column = lax.broadcasted_iota(jnp.int32, (8 * chunks, each * chunks), 1)
    turn_back = (gather_row % 8 * chunks + gather_row // 8 == gather_column).astype(bf16)
    loads[2].wait()
    loads[3].wait()
    base_copy.wait_recv()
    base_own[...] = base_own[...] + base_in[...]

    part_copies = []
    delta_copies = {}

    def shrink(g):
        group = groups[g]
        blocks = pl.ds(group[0], each)
        for k in group:
            if k > 0:
                row_copies[k].wait_recv()
        turned = dot(turn_back, rows_in[blocks, main:, :].reshape(each * chunks, 128))
        taken = [
            jnp.concatenate(
                [
                    rows_in[blocks, c * BLOCK : (c + 1) * BLOCK, :].reshape(count, 128),
                    turned[c * 8 : (c + 1) * 8].astype(bf16),
                ],
                axis=0,
            )
            for c in range(chunks)
        ]
        part = lax.dot_general(
            jnp.concatenate(taken, axis=1), down[...], (((1,), (1,)), ((), ())),
            preferred_element_type=f32,
        )
        part_out[g] = jnp.concatenate([part, jnp.zeros((count + 8, 128 - rank), f32)], axis=1)
        part_copies.append(
            push(part_out.at[g], part_in.at[g], part_sem, g, {"tensor": 1 - core})
        )

    def widen(g):
        part_copies[g].wait_recv()
        reduced = (part_out[g] + part_in[g])[:, :rank]
        stacked = jnp.concatenate([x.astype(f32) for x in three_parts(reduced)], axis=0)
        wide = dot(stacked.astype(bf16), up[...])
        size = count + 8
        wide = wide[:size] + wide[size : 2 * size] + wide[2 * size :]
        for i, k in enumerate(groups[g]):
            target = delta_in if k == 0 else delta_out
            if k == 0:
                delta_in[0] = jnp.zeros((SLOTS, 128), f32)
            target[k, :BLOCK] = wide[i * BLOCK : (i + 1) * BLOCK, :128]
            target[k, BLOCK : 2 * BLOCK] = wide[i * BLOCK : (i + 1) * BLOCK, 128:]
            target[k, 2 * BLOCK : 2 * BLOCK + 1] = wide[count + i : count + i + 1, :128]
            target[k, 2 * BLOCK + 1 : 2 * BLOCK + 2] = wide[count + i : count + i + 1, 128:]
            if k > 0:
                delta_copies[k] = push(
                    delta_out.at[k], delta_in.at[k], delta_sem, k, {"adapter": me ^ k}
                )

    for g in range(len(groups)):
        shrink(g)
        if g > 0:
            widen(g - 1)
    widen(len(groups) - 1)

    total = base_own[...]
    for group, back in zip(groups, backs):
        for k in group:
            if k > 0:
                delta_copies[k].wait_recv()
        parts = three_parts(
            delta_in[group[0] : group[0] + each].reshape(each * SLOTS, 128)
        )
        total = total + jnp.concatenate(
            [sum(dot(side, x) for x in parts) for side in back], axis=1
        )
    out_ref[...] = total.astype(out_ref.dtype)

    for copy in sent:
        copy.wait_send()


GROUPS = ((0,), (1,), (2,), (3,), (4,), (5,), (6,), (7,))
SLOTS = 2 * BLOCK + 8


def fused_body(
    hidden_state_rows, value_weight, adapter_down_weight, adapter_up_weight, request_adapter_index
):
    n = lax.axis_size("adapter")
    rows, depth = hidden_state_rows.shape
    width = value_weight.shape[1]
    half = width // 2
    rank = adapter_down_weight.shape[2]
    chunks = depth // 128
    each = len(GROUPS[0])
    dma = pltpu.SemaphoreType.DMA
    return pl.pallas_call(
        functools.partial(adapter_kernel, n, GROUPS),
        out_shape=jax.ShapeDtypeStruct((rows, half), bf16),
        in_specs=[pl.BlockSpec(memory_space=pl.ANY)] * 5,
        out_specs=pl.BlockSpec(memory_space=pltpu.VMEM),
        scratch_shapes=[
            pltpu.VMEM((1, rows), jnp.int32),
            pltpu.VMEM((rows, depth), bf16),
            pltpu.VMEM((depth, width), bf16),
            pltpu.VMEM((rank, depth), bf16),
            pltpu.VMEM((rank, half), bf16),
            pltpu.VMEM((n, chunks * (BLOCK + 1), 128), bf16),
            pltpu.VMEM((n, chunks * (BLOCK + 1), 128), bf16),
            pltpu.VMEM((n // each, each * BLOCK + 8, 128), f32),
            pltpu.VMEM((n // each, each * BLOCK + 8, 128), f32),
            pltpu.VMEM((n, SLOTS, 128), f32),
            pltpu.VMEM((n, SLOTS, 128), f32),
            pltpu.VMEM((rows, half), f32),
            pltpu.VMEM((rows, half), f32),
            pltpu.VMEM((rows, half), f32),
            dma((5,)),
            dma((2, n)),
            dma((2, n // each)),
            dma((2, n)),
            dma((2, 1)),
        ],
        compiler_params=pltpu.CompilerParams(
            collective_id=0, has_side_effects=True, vmem_limit_bytes=60 * 1024 * 1024
        ),
    )(
        request_adapter_index.reshape(1, rows),
        hidden_state_rows,
        value_weight,
        jnp.swapaxes(adapter_down_weight.reshape(depth, rank), 0, 1),
        adapter_up_weight.reshape(rank, half),
    )


def adapter_delta_rows(incoming_rows, down_matrix, up_matrix):
    flat_rows = incoming_rows.reshape(-1, incoming_rows.shape[-1])
    reduced_rows = jnp.dot(flat_rows, down_matrix, preferred_element_type=jnp.float32)
    reduced_rows = lax.psum(reduced_rows, "tensor")
    widened_rows = jnp.dot(
        reduced_rows, up_matrix, precision=highest_precision, preferred_element_type=jnp.float32
    )
    widened_rows = widened_rows.reshape(
        incoming_rows.shape[0], incoming_rows.shape[1], up_matrix.shape[1]
    )
    return lax.all_to_all(widened_rows, "adapter", split_axis=0, concat_axis=0, tiled=True)


def general_body(
    hidden_state_rows, value_weight, adapter_down_weight, adapter_up_weight, request_adapter_index
):
    holders = lax.axis_size("adapter")
    rows_here = hidden_state_rows.shape[0]
    slots_per_pair = 2 + (rows_here - 1) // holders
    holder_ids = lax.broadcasted_iota(jnp.int32, (rows_here, holders), 1)
    onehot = (request_adapter_index[:, None] == holder_ids).astype(jnp.int32)
    pair_ranks = jnp.sum(onehot * (jnp.cumsum(onehot, axis=0) - 1), axis=1)
    slot_index = request_adapter_index * slots_per_pair + pair_ranks
    down_matrix = adapter_down_weight[0]
    up_matrix = adapter_up_weight[0].astype(jnp.float32)
    slot_ids = lax.broadcasted_iota(jnp.int32, (holders * slots_per_pair, rows_here), 0)
    placing = (slot_ids == slot_index[None, :]).astype(hidden_state_rows.dtype)
    send_rows = jnp.dot(placing, hidden_state_rows, preferred_element_type=jnp.float32).astype(
        hidden_state_rows.dtype
    )
    send_rows = send_rows.reshape(holders, slots_per_pair, hidden_state_rows.shape[1])
    value_result = adapter_delta_rows(
        lax.all_to_all(send_rows, "adapter", split_axis=0, concat_axis=0, tiled=True),
        down_matrix,
        up_matrix,
    )
    delta_rows = jnp.take(value_result.reshape(holders * slots_per_pair, -1), slot_index, axis=0)
    base_terms = jnp.dot(hidden_state_rows, value_weight, preferred_element_type=jnp.float32)
    own_columns = lax.psum_scatter(base_terms, "tensor", scatter_dimension=1, tiled=True)
    summed = own_columns + delta_rows
    return summed.astype(jnp.bfloat16)


def body(*arrays):
    n = lax.axis_size("adapter")
    if n == 8 and arrays[0].shape[0] == n * BLOCK:
        return fused_body(*arrays)
    return general_body(*arrays)


def solution(mesh):
    return jax.shard_map(
        body,
        mesh=mesh,
        in_specs=(
            P(("groups", "adapter"), "tensor"),
            P("tensor", None),
            P(("groups", "adapter"), "tensor", None),
            P(("groups", "adapter"), None, "tensor"),
            P(("groups", "adapter")),
        ),
        out_specs=P(("groups", "adapter"), "tensor"),
        check_vma=False,
    )
```

```python
import functools

import jax
import jax.numpy as jnp
from jax import lax
from jax.experimental import pallas as pl
from jax.experimental.pallas import tpu as pltpu
from jax.sharding import PartitionSpec as P

highest_precision = lax.Precision.HIGHEST
BLOCK = 16
f32 = jnp.float32
bf16 = jnp.bfloat16


def dot(a, b):
    return jnp.dot(a, b, preferred_element_type=f32)


def three_parts(x):
    high = x.astype(bf16)
    rest = x - high.astype(f32)
    middle = rest.astype(bf16)
    low = (rest - middle.astype(f32)).astype(bf16)
    return high, middle, low


def adapter_kernel(
    n, groups, index_hbm, hidden_hbm, value_hbm, down_hbm, up_hbm, out_ref,
    index, hidden, value, down, up, rows_out, rows_in, part_out, part_in, delta_out, delta_in,
    base_own, base_out, base_in,
    load_sem, rows_sem, part_sem, delta_sem, base_sem,
):
    me = lax.axis_index("adapter")
    core = lax.axis_index("tensor")
    rows, depth = hidden.shape
    width = value.shape[1]
    half = width // 2
    rank = up.shape[0]
    chunks = depth // 128
    main = chunks * BLOCK
    each = len(groups[0])
    count = each * BLOCK

    loads = [
        pltpu.make_async_copy(src, dst, load_sem.at[i])
        for i, (src, dst) in enumerate(
            (
                (index_hbm, index), (hidden_hbm, hidden), (down_hbm, down), (up_hbm, up),
                (value_hbm, value),
            )
        )
    ]
    loads[0].start()
    loads[1].start()
    delta_in[:, 2 * BLOCK :] = jnp.zeros((n, SLOTS - 2 * BLOCK, 128), f32)

    barrier = pltpu.get_barrier_semaphore()
    for k in range(1, n):
        pl.semaphore_signal(barrier, inc=1, device_id={"adapter": me ^ k})
    pl.semaphore_signal(barrier, inc=1, device_id={"tensor": 1 - core})

    sent = []

    def push(src, dst, sems, k, target):
        copy = pltpu.make_async_remote_copy(
            src_ref=src, dst_ref=dst, send_sem=sems.at[0, k], recv_sem=sems.at[1, k],
            device_id=target,
        )
        copy.start()
        sent.append(copy)
        return copy

    loads[0].wait()
    block_of = index[...] ^ me
    member = (lax.broadcasted_iota(jnp.int32, (n, rows), 0) == block_of).astype(f32)
    earlier = (
        lax.broadcasted_iota(jnp.int32, (rows, rows), 0)
        < lax.broadcasted_iota(jnp.int32, (rows, rows), 1)
    ).astype(bf16)
    place = jnp.sum(member * dot(member.astype(bf16), earlier), axis=0, keepdims=True)
    place = place.astype(jnp.int32)
    main_slot = jnp.where(place < BLOCK, block_of * BLOCK + place, -1)
    spill_block = jnp.where(place == BLOCK, block_of, -1)
    main_pick = lax.broadcasted_iota(jnp.int32, (n * BLOCK, rows), 0) == main_slot
    spill_pick = lax.broadcasted_iota(jnp.int32, (n, rows), 0) == spill_block
    pick = jnp.concatenate([main_pick.astype(f32), spill_pick.astype(f32)], axis=0).astype(bf16)
    turn_row = lax.broadcasted_iota(jnp.int32, (n * chunks, n * chunks), 0)
    turn_column = lax.broadcasted_iota(jnp.int32, (n * chunks, n * chunks), 1)
    turn = (turn_row % chunks * n + turn_row // chunks == turn_column).astype(bf16)

    loads[1].wait()
    for load in loads[2:]:
        load.start()
    picked = dot(pick, hidden[...])
    for c in range(chunks):
        rows_out[:, c * BLOCK : (c + 1) * BLOCK, :] = (
            picked[: n * BLOCK, c * 128 : (c + 1) * 128].astype(bf16).reshape(n, BLOCK, 128)
        )
    spilled = jnp.concatenate(
        [picked[n * BLOCK :, c * 128 : (c + 1) * 128] for c in range(chunks)], axis=0
    ).astype(bf16)
    rows_out[:, main:, :] = dot(turn, spilled).astype(bf16).reshape(n, chunks, 128)

    pl.semaphore_wait(barrier, n)
    row_copies = {}
    for k in range(1, n):
        row_copies[k] = push(rows_out.at[k], rows_in.at[k], rows_sem, k, {"adapter": me ^ k})

    loads[4].wait()
    base = dot(hidden[...], value[...])
    first, second = base[:, :half], base[:, half:]
    base_own[...] = jnp.where(core == 0, first, second)
    base_out[...] = jnp.where(core == 0, second, first)
    base_copy = push(base_out, base_in, base_sem, 0, {"tensor": 1 - core})

    rows_in[0] = rows_out[0]
    delta_out[...] = jnp.zeros_like(delta_out)
    low_slot = jnp.where(place < BLOCK, place, 2 * BLOCK) + block_of * SLOTS
    high_slot = jnp.where(place < BLOCK, BLOCK + place, 2 * BLOCK + 1) + block_of * SLOTS
    slot_ids = lax.broadcasted_iota(jnp.int32, (128, rows), 0)
    backs = []
    for group in groups:
        slots = jnp.where(slot_ids < each * SLOTS, slot_ids + group[0] * SLOTS, -1)
        backs.append(
            [
                jnp.transpose((slots == slot).astype(f32))[:, : each * SLOTS].astype(bf16)
                for slot in (low_slot, high_slot)
            ]
        )
    gather_row = lax.broadcasted_iota(jnp.int32, (8 * chunks, each * chunks), 0)
    gather_column = lax.broadcasted_iota(jnp.int32, (8 * chunks, each * chunks), 1)
    turn_back = (gather_row % 8 * chunks + gather_row // 8 == gather_column).astype(bf16)
    loads[2].wait()
    loads[3].wait()
    base_copy.wait_recv()
    base_own[...] = base_own[...] + base_in[...]

    part_copies = []
    delta_copies = {}

    def shrink(g):
        group = groups[g]
        blocks = pl.ds(group[0], each)
        for k in group:
            if k > 0:
                row_copies[k].wait_recv()
        turned = dot(turn_back, rows_in[blocks, main:, :].reshape(each * chunks, 128))
        taken = [
            jnp.concatenate(
                [
                    rows_in[blocks, c * BLOCK : (c + 1) * BLOCK, :].reshape(count, 128),
                    turned[c * 8 : (c + 1) * 8].astype(bf16),
                ],
                axis=0,
            )
            for c in range(chunks)
        ]
        part = lax.dot_general(
            jnp.concatenate(taken, axis=1), down[...], (((1,), (1,)), ((), ())),
            preferred_element_type=f32,
        )
        part_out[g] = jnp.concatenate([part, jnp.zeros((count + 8, 128 - rank), f32)], axis=1)
        part_copies.append(
            push(part_out.at[g], part_in.at[g], part_sem, g, {"tensor": 1 - core})
        )

    def widen(g):
        part_copies[g].wait_recv()
        reduced = (part_out[g] + part_in[g])[:, :rank]
        stacked = jnp.concatenate([x.astype(f32) for x in three_parts(reduced)], axis=0)
        wide = dot(stacked.astype(bf16), up[...])
        size = count + 8
        wide = wide[:size] + wide[size : 2 * size] + wide[2 * size :]
        for i, k in enumerate(groups[g]):
            target = delta_in if k == 0 else delta_out
            if k == 0:
                delta_in[0] = jnp.zeros((SLOTS, 128), f32)
            target[k, :BLOCK] = wide[i * BLOCK : (i + 1) * BLOCK, :128]
            target[k, BLOCK : 2 * BLOCK] = wide[i * BLOCK : (i + 1) * BLOCK, 128:]
            target[k, 2 * BLOCK : 2 * BLOCK + 1] = wide[count + i : count + i + 1, :128]
            target[k, 2 * BLOCK + 1 : 2 * BLOCK + 2] = wide[count + i : count + i + 1, 128:]
            if k > 0:
                delta_copies[k] = push(
                    delta_out.at[k, :FILLED], delta_in.at[k, :FILLED], delta_sem, k, {"adapter": me ^ k}
                )

    for g in range(len(groups)):
        shrink(g)
        if g > 0:
            widen(g - 1)
    widen(len(groups) - 1)

    total = base_own[...]
    for group, back in zip(groups, backs):
        for k in group:
            if k > 0:
                delta_copies[k].wait_recv()
        parts = three_parts(
            delta_in[group[0] : group[0] + each].reshape(each * SLOTS, 128)
        )
        total = total + jnp.concatenate(
            [sum(dot(side, x) for x in parts) for side in back], axis=1
        )
    out_ref[...] = total.astype(out_ref.dtype)

    for copy in sent:
        copy.wait_send()


GROUPS = ((0,), (1,), (2,), (3,), (4,), (5,), (6,), (7,))
SLOTS = 2 * BLOCK + 8
FILLED = 2 * BLOCK + 2


def fused_body(
    hidden_state_rows, value_weight, adapter_down_weight, adapter_up_weight, request_adapter_index
):
    n = lax.axis_size("adapter")
    rows, depth = hidden_state_rows.shape
    width = value_weight.shape[1]
    half = width // 2
    rank = adapter_down_weight.shape[2]
    chunks = depth // 128
    each = len(GROUPS[0])
    dma = pltpu.SemaphoreType.DMA
    return pl.pallas_call(
        functools.partial(adapter_kernel, n, GROUPS),
        out_shape=jax.ShapeDtypeStruct((rows, half), bf16),
        in_specs=[pl.BlockSpec(memory_space=pl.ANY)] * 5,
        out_specs=pl.BlockSpec(memory_space=pltpu.VMEM),
        scratch_shapes=[
            pltpu.VMEM((1, rows), jnp.int32),
            pltpu.VMEM((rows, depth), bf16),
            pltpu.VMEM((depth, width), bf16),
            pltpu.VMEM((rank, depth), bf16),
            pltpu.VMEM((rank, half), bf16),
            pltpu.VMEM((n, chunks * (BLOCK + 1), 128), bf16),
            pltpu.VMEM((n, chunks * (BLOCK + 1), 128), bf16),
            pltpu.VMEM((n // each, each * BLOCK + 8, 128), f32),
            pltpu.VMEM((n // each, each * BLOCK + 8, 128), f32),
            pltpu.VMEM((n, SLOTS, 128), f32),
            pltpu.VMEM((n, SLOTS, 128), f32),
            pltpu.VMEM((rows, half), f32),
            pltpu.VMEM((rows, half), f32),
            pltpu.VMEM((rows, half), f32),
            dma((5,)),
            dma((2, n)),
            dma((2, n // each)),
            dma((2, n)),
            dma((2, 1)),
        ],
        compiler_params=pltpu.CompilerParams(
            collective_id=0, has_side_effects=True, vmem_limit_bytes=60 * 1024 * 1024
        ),
    )(
        request_adapter_index.reshape(1, rows),
        hidden_state_rows,
        value_weight,
        jnp.swapaxes(adapter_down_weight.reshape(depth, rank), 0, 1),
        adapter_up_weight.reshape(rank, half),
    )


def adapter_delta_rows(incoming_rows, down_matrix, up_matrix):
    flat_rows = incoming_rows.reshape(-1, incoming_rows.shape[-1])
    reduced_rows = jnp.dot(flat_rows, down_matrix, preferred_element_type=jnp.float32)
    reduced_rows = lax.psum(reduced_rows, "tensor")
    widened_rows = jnp.dot(
        reduced_rows, up_matrix, precision=highest_precision, preferred_element_type=jnp.float32
    )
    widened_rows = widened_rows.reshape(
        incoming_rows.shape[0], incoming_rows.shape[1], up_matrix.shape[1]
    )
    return lax.all_to_all(widened_rows, "adapter", split_axis=0, concat_axis=0, tiled=True)


def general_body(
    hidden_state_rows, value_weight, adapter_down_weight, adapter_up_weight, request_adapter_index
):
    holders = lax.axis_size("adapter")
    rows_here = hidden_state_rows.shape[0]
    slots_per_pair = 2 + (rows_here - 1) // holders
    holder_ids = lax.broadcasted_iota(jnp.int32, (rows_here, holders), 1)
    onehot = (request_adapter_index[:, None] == holder_ids).astype(jnp.int32)
    pair_ranks = jnp.sum(onehot * (jnp.cumsum(onehot, axis=0) - 1), axis=1)
    slot_index = request_adapter_index * slots_per_pair + pair_ranks
    down_matrix = adapter_down_weight[0]
    up_matrix = adapter_up_weight[0].astype(jnp.float32)
    slot_ids = lax.broadcasted_iota(jnp.int32, (holders * slots_per_pair, rows_here), 0)
    placing = (slot_ids == slot_index[None, :]).astype(hidden_state_rows.dtype)
    send_rows = jnp.dot(placing, hidden_state_rows, preferred_element_type=jnp.float32).astype(
        hidden_state_rows.dtype
    )
    send_rows = send_rows.reshape(holders, slots_per_pair, hidden_state_rows.shape[1])
    value_result = adapter_delta_rows(
        lax.all_to_all(send_rows, "adapter", split_axis=0, concat_axis=0, tiled=True),
        down_matrix,
        up_matrix,
    )
    delta_rows = jnp.take(value_result.reshape(holders * slots_per_pair, -1), slot_index, axis=0)
    base_terms = jnp.dot(hidden_state_rows, value_weight, preferred_element_type=jnp.float32)
    own_columns = lax.psum_scatter(base_terms, "tensor", scatter_dimension=1, tiled=True)
    summed = own_columns + delta_rows
    return summed.astype(jnp.bfloat16)


def body(*arrays):
    n = lax.axis_size("adapter")
    if n == 8 and arrays[0].shape[0] == n * BLOCK:
        return fused_body(*arrays)
    return general_body(*arrays)


def solution(mesh):
    return jax.shard_map(
        body,
        mesh=mesh,
        in_specs=(
            P(("groups", "adapter"), "tensor"),
            P("tensor", None),
            P(("groups", "adapter"), "tensor", None),
            P(("groups", "adapter"), None, "tensor"),
            P(("groups", "adapter")),
        ),
        out_specs=P(("groups", "adapter"), "tensor"),
        check_vma=False,
    )
```

```python
import functools

import jax
import jax.numpy as jnp
from jax import lax
from jax.experimental import pallas as pl
from jax.experimental.pallas import tpu as pltpu
from jax.sharding import PartitionSpec as P

highest_precision = lax.Precision.HIGHEST
BLOCK = 16
f32 = jnp.float32
bf16 = jnp.bfloat16


def dot(a, b):
    return jnp.dot(a, b, preferred_element_type=f32)


def three_parts(x):
    high = x.astype(bf16)
    rest = x - high.astype(f32)
    middle = rest.astype(bf16)
    low = (rest - middle.astype(f32)).astype(bf16)
    return high, middle, low


def adapter_kernel(
    n, groups, index_hbm, hidden_hbm, value_hbm, down_hbm, up_hbm, out_ref,
    index, hidden, value, down, up, rows_out, rows_in, part_out, part_in, delta_out, delta_in,
    base_own, base_out, base_in,
    load_sem, rows_sem, part_sem, delta_sem, base_sem,
):
    me = lax.axis_index("adapter")
    core = lax.axis_index("tensor")
    rows, depth = hidden.shape
    width = value.shape[1]
    half = width // 2
    rank = up.shape[0]
    chunks = depth // 128
    main = chunks * BLOCK
    each = len(groups[0])
    count = each * BLOCK

    loads = [
        pltpu.make_async_copy(src, dst, load_sem.at[i])
        for i, (src, dst) in enumerate(
            (
                (index_hbm, index), (hidden_hbm, hidden), (down_hbm, down), (up_hbm, up),
                (value_hbm, value),
            )
        )
    ]
    loads[0].start()
    loads[1].start()
    delta_in[:, 2 * BLOCK :] = jnp.zeros((n, SLOTS - 2 * BLOCK, 128), f32)

    barrier = pltpu.get_barrier_semaphore()
    for k in range(1, n):
        pl.semaphore_signal(barrier, inc=1, device_id={"adapter": me ^ k})
    pl.semaphore_signal(barrier, inc=1, device_id={"tensor": 1 - core})

    sent = []

    def push(src, dst, sems, k, target):
        copy = pltpu.make_async_remote_copy(
            src_ref=src, dst_ref=dst, send_sem=sems.at[0, k], recv_sem=sems.at[1, k],
            device_id=target,
        )
        copy.start()
        sent.append(copy)
        return copy

    loads[0].wait()
    block_of = index[...] ^ me
    member = (lax.broadcasted_iota(jnp.int32, (n, rows), 0) == block_of).astype(f32)
    earlier = (
        lax.broadcasted_iota(jnp.int32, (rows, rows), 0)
        < lax.broadcasted_iota(jnp.int32, (rows, rows), 1)
    ).astype(bf16)
    place = jnp.sum(member * dot(member.astype(bf16), earlier), axis=0, keepdims=True)
    place = place.astype(jnp.int32)
    main_slot = jnp.where(place < BLOCK, block_of * BLOCK + place, -1)
    spill_block = jnp.where(place == BLOCK, block_of, -1)
    main_pick = lax.broadcasted_iota(jnp.int32, (n * BLOCK, rows), 0) == main_slot
    spill_pick = lax.broadcasted_iota(jnp.int32, (n, rows), 0) == spill_block
    pick = jnp.concatenate([main_pick.astype(f32), spill_pick.astype(f32)], axis=0).astype(bf16)
    turn_row = lax.broadcasted_iota(jnp.int32, (n * chunks, n * chunks), 0)
    turn_column = lax.broadcasted_iota(jnp.int32, (n * chunks, n * chunks), 1)
    turn = (turn_row % chunks * n + turn_row // chunks == turn_column).astype(bf16)

    loads[1].wait()
    for load in loads[2:]:
        load.start()
    row_copies = {}
    spilled = []
    for part in range(2):
        first, last = part * chunks // 2, (part + 1) * chunks // 2
        picked = dot(pick, hidden[:, first * 128 : last * 128])
        for c in range(first, last):
            piece = picked[:, (c - first) * 128 : (c - first + 1) * 128]
            rows_out[:, c * BLOCK : (c + 1) * BLOCK, :] = (
                piece[: n * BLOCK].astype(bf16).reshape(n, BLOCK, 128)
            )
            spilled.append(piece[n * BLOCK :])
        if part == 0:
            pl.semaphore_wait(barrier, n)
            region = pl.ds(0, main // 2)
        else:
            turned = dot(turn, jnp.concatenate(spilled, axis=0).astype(bf16))
            rows_out[:, main:, :] = turned.astype(bf16).reshape(n, chunks, 128)
            region = pl.ds(main // 2, main // 2 + chunks)
        for k in range(1, n):
            row_copies[part * n + k] = push(
                rows_out.at[k, region], rows_in.at[k, region], rows_sem, part * n + k,
                {"adapter": me ^ k},
            )

    loads[4].wait()
    base = dot(hidden[...], value[...])
    first, second = base[:, :half], base[:, half:]
    base_own[...] = jnp.where(core == 0, first, second)
    base_out[...] = jnp.where(core == 0, second, first)
    base_copy = push(base_out, base_in, base_sem, 0, {"tensor": 1 - core})

    rows_in[0] = rows_out[0]
    delta_out[...] = jnp.zeros_like(delta_out)
    low_slot = jnp.where(place < BLOCK, place, 2 * BLOCK) + block_of * SLOTS
    high_slot = jnp.where(place < BLOCK, BLOCK + place, 2 * BLOCK + 1) + block_of * SLOTS
    slot_ids = lax.broadcasted_iota(jnp.int32, (128, rows), 0)
    backs = []
    for group in groups:
        slots = jnp.where(slot_ids < each * SLOTS, slot_ids + group[0] * SLOTS, -1)
        backs.append(
            [
                jnp.transpose((slots == slot).astype(f32))[:, : each * SLOTS].astype(bf16)
                for slot in (low_slot, high_slot)
            ]
        )
    gather_row = lax.broadcasted_iota(jnp.int32, (8 * chunks, each * chunks), 0)
    gather_column = lax.broadcasted_iota(jnp.int32, (8 * chunks, each * chunks), 1)
    turn_back = (gather_row % 8 * chunks + gather_row // 8 == gather_column).astype(bf16)
    loads[2].wait()
    loads[3].wait()
    base_copy.wait_recv()
    base_own[...] = base_own[...] + base_in[...]

    part_copies = []
    delta_copies = {}

    def shrink(g):
        group = groups[g]
        blocks = pl.ds(group[0], each)
        for k in group:
            if k > 0:
                row_copies[k].wait_recv()
                row_copies[n + k].wait_recv()
        turned = dot(turn_back, rows_in[blocks, main:, :].reshape(each * chunks, 128))
        taken = [
            jnp.concatenate(
                [
                    rows_in[blocks, c * BLOCK : (c + 1) * BLOCK, :].reshape(count, 128),
                    turned[c * 8 : (c + 1) * 8].astype(bf16),
                ],
                axis=0,
            )
            for c in range(chunks)
        ]
        part = lax.dot_general(
            jnp.concatenate(taken, axis=1), down[...], (((1,), (1,)), ((), ())),
            preferred_element_type=f32,
        )
        part_out[g] = jnp.concatenate([part, jnp.zeros((count + 8, 128 - rank), f32)], axis=1)
        part_copies.append(
            push(part_out.at[g], part_in.at[g], part_sem, g, {"tensor": 1 - core})
        )

    def widen(g):
        part_copies[g].wait_recv()
        reduced = (part_out[g] + part_in[g])[:, :rank]
        stacked = jnp.concatenate([x.astype(f32) for x in three_parts(reduced)], axis=0)
        wide = dot(stacked.astype(bf16), up[...])
        size = count + 8
        wide = wide[:size] + wide[size : 2 * size] + wide[2 * size :]
        for i, k in enumerate(groups[g]):
            target = delta_in if k == 0 else delta_out
            if k == 0:
                delta_in[0] = jnp.zeros((SLOTS, 128), f32)
            target[k, :BLOCK] = wide[i * BLOCK : (i + 1) * BLOCK, :128]
            target[k, BLOCK : 2 * BLOCK] = wide[i * BLOCK : (i + 1) * BLOCK, 128:]
            target[k, 2 * BLOCK : 2 * BLOCK + 1] = wide[count + i : count + i + 1, :128]
            target[k, 2 * BLOCK + 1 : 2 * BLOCK + 2] = wide[count + i : count + i + 1, 128:]
            if k > 0:
                delta_copies[k] = push(
                    delta_out.at[k, :FILLED], delta_in.at[k, :FILLED], delta_sem, k, {"adapter": me ^ k}
                )

    for g in range(len(groups)):
        shrink(g)
        if g > 0:
            widen(g - 1)
    widen(len(groups) - 1)

    total = base_own[...]
    for group, back in zip(groups, backs):
        for k in group:
            if k > 0:
                delta_copies[k].wait_recv()
        parts = three_parts(
            delta_in[group[0] : group[0] + each].reshape(each * SLOTS, 128)
        )
        total = total + jnp.concatenate(
            [sum(dot(side, x) for x in parts) for side in back], axis=1
        )
    out_ref[...] = total.astype(out_ref.dtype)

    for copy in sent:
        copy.wait_send()


GROUPS = ((0,), (1,), (2,), (3,), (4,), (5,), (6,), (7,))
SLOTS = 2 * BLOCK + 8
FILLED = 2 * BLOCK + 2


def fused_body(
    hidden_state_rows, value_weight, adapter_down_weight, adapter_up_weight, request_adapter_index
):
    n = lax.axis_size("adapter")
    rows, depth = hidden_state_rows.shape
    width = value_weight.shape[1]
    half = width // 2
    rank = adapter_down_weight.shape[2]
    chunks = depth // 128
    each = len(GROUPS[0])
    dma = pltpu.SemaphoreType.DMA
    return pl.pallas_call(
        functools.partial(adapter_kernel, n, GROUPS),
        out_shape=jax.ShapeDtypeStruct((rows, half), bf16),
        in_specs=[pl.BlockSpec(memory_space=pl.ANY)] * 5,
        out_specs=pl.BlockSpec(memory_space=pltpu.VMEM),
        scratch_shapes=[
            pltpu.VMEM((1, rows), jnp.int32),
            pltpu.VMEM((rows, depth), bf16),
            pltpu.VMEM((depth, width), bf16),
            pltpu.VMEM((rank, depth), bf16),
            pltpu.VMEM((rank, half), bf16),
            pltpu.VMEM((n, chunks * (BLOCK + 1), 128), bf16),
            pltpu.VMEM((n, chunks * (BLOCK + 1), 128), bf16),
            pltpu.VMEM((n // each, each * BLOCK + 8, 128), f32),
            pltpu.VMEM((n // each, each * BLOCK + 8, 128), f32),
            pltpu.VMEM((n, SLOTS, 128), f32),
            pltpu.VMEM((n, SLOTS, 128), f32),
            pltpu.VMEM((rows, half), f32),
            pltpu.VMEM((rows, half), f32),
            pltpu.VMEM((rows, half), f32),
            dma((5,)),
            dma((2, 2 * n)),
            dma((2, n // each)),
            dma((2, n)),
            dma((2, 1)),
        ],
        compiler_params=pltpu.CompilerParams(
            collective_id=0, has_side_effects=True, vmem_limit_bytes=60 * 1024 * 1024
        ),
    )(
        request_adapter_index.reshape(1, rows),
        hidden_state_rows,
        value_weight,
        jnp.swapaxes(adapter_down_weight.reshape(depth, rank), 0, 1),
        adapter_up_weight.reshape(rank, half),
    )


def adapter_delta_rows(incoming_rows, down_matrix, up_matrix):
    flat_rows = incoming_rows.reshape(-1, incoming_rows.shape[-1])
    reduced_rows = jnp.dot(flat_rows, down_matrix, preferred_element_type=jnp.float32)
    reduced_rows = lax.psum(reduced_rows, "tensor")
    widened_rows = jnp.dot(
        reduced_rows, up_matrix, precision=highest_precision, preferred_element_type=jnp.float32
    )
    widened_rows = widened_rows.reshape(
        incoming_rows.shape[0], incoming_rows.shape[1], up_matrix.shape[1]
    )
    return lax.all_to_all(widened_rows, "adapter", split_axis=0, concat_axis=0, tiled=True)


def general_body(
    hidden_state_rows, value_weight, adapter_down_weight, adapter_up_weight, request_adapter_index
):
    holders = lax.axis_size("adapter")
    rows_here = hidden_state_rows.shape[0]
    slots_per_pair = 2 + (rows_here - 1) // holders
    holder_ids = lax.broadcasted_iota(jnp.int32, (rows_here, holders), 1)
    onehot = (request_adapter_index[:, None] == holder_ids).astype(jnp.int32)
    pair_ranks = jnp.sum(onehot * (jnp.cumsum(onehot, axis=0) - 1), axis=1)
    slot_index = request_adapter_index * slots_per_pair + pair_ranks
    down_matrix = adapter_down_weight[0]
    up_matrix = adapter_up_weight[0].astype(jnp.float32)
    slot_ids = lax.broadcasted_iota(jnp.int32, (holders * slots_per_pair, rows_here), 0)
    placing = (slot_ids == slot_index[None, :]).astype(hidden_state_rows.dtype)
    send_rows = jnp.dot(placing, hidden_state_rows, preferred_element_type=jnp.float32).astype(
        hidden_state_rows.dtype
    )
    send_rows = send_rows.reshape(holders, slots_per_pair, hidden_state_rows.shape[1])
    value_result = adapter_delta_rows(
        lax.all_to_all(send_rows, "adapter", split_axis=0, concat_axis=0, tiled=True),
        down_matrix,
        up_matrix,
    )
    delta_rows = jnp.take(value_result.reshape(holders * slots_per_pair, -1), slot_index, axis=0)
    base_terms = jnp.dot(hidden_state_rows, value_weight, preferred_element_type=jnp.float32)
    own_columns = lax.psum_scatter(base_terms, "tensor", scatter_dimension=1, tiled=True)
    summed = own_columns + delta_rows
    return summed.astype(jnp.bfloat16)


def body(*arrays):
    n = lax.axis_size("adapter")
    if n == 8 and arrays[0].shape[0] == n * BLOCK:
        return fused_body(*arrays)
    return general_body(*arrays)


def solution(mesh):
    return jax.shard_map(
        body,
        mesh=mesh,
        in_specs=(
            P(("groups", "adapter"), "tensor"),
            P("tensor", None),
            P(("groups", "adapter"), "tensor", None),
            P(("groups", "adapter"), None, "tensor"),
            P(("groups", "adapter")),
        ),
        out_specs=P(("groups", "adapter"), "tensor"),
        check_vma=False,
    )
```
